256 devices in a mesh: tensor: 4 (over y_hi, core), dp: 8 (over z), replica: 8 (over x, y_lo).
Axes of the slice: x: 4, y: 4 (y_hi: 2, y_lo: 2; y = y_hi * 2 + y_lo), z: 8, core: 2. Of those that a mesh axis runs over, the one named last changes fastest.
Arguments:
- features: bfloat16 [49152, 8192], P(('dp', 'replica'), 'tensor'), may hold values from -130 to 130
- cotangent: bfloat16 [49152, 1024], P(('dp', 'replica'), 'tensor'), may hold values from -45 to 45
- master: float32 [8192, 1024], P('dp', 'tensor'), may hold values from -6 to 6
- first: float32 [8192, 1024], P('dp', 'tensor'), may hold values from -3 to 3
- second: float32 [8192, 1024], P('dp', 'tensor'), may hold values from 0.05 to 2
Outputs:
- new_master: float32 [8192, 1024], P('dp', 'tensor')
- new_first: float32 [8192, 1024], P('dp', 'tensor')
- new_second: float32 [8192, 1024], P('dp', 'tensor')
The draws below stay inside these ranges and needn't reach their ends.
All inputs are finite; a program needn't handle non-finite values.
Results may differ from the reference program's by a relative error of at most 0.0003.
Values may be sent and summed in bfloat16 or wider, within the bound.
No kernel may reach another device: no remote copies, remote signals or barrier semaphores. Data moves between devices by JAX's collectives and lax.ppermute only.
A program may use at most 128 MiB of HBM per device.

```python
import math
import jax
import jax.numpy as jnp
from jax import lax

D = 8192
COLS = 1024
TOK_DEV = 768
TOKENS = 49152


def scaled_normal(key, rows, cols, rising):
    key_base, key_cols, key_rows = jax.random.split(key, 3)
    base = jnp.clip(jax.random.normal(key_base, (rows, cols), jnp.float32), -4.0, 4.0)
    col_scale = jnp.exp(jax.random.uniform(key_cols, (1, cols), jnp.float32, -1.15, 1.15))
    col_scale = col_scale * jnp.exp(rising * jnp.arange(cols, dtype=jnp.float32) / cols)
    row_scale = jnp.exp(jax.random.uniform(key_rows, (rows, 1), jnp.float32, -1.15, 1.15))
    return base * col_scale * row_scale


def draw_features(key, part):
    key = jax.random.fold_in(key, 11)
    values = scaled_normal(key, TOKENS, D, 1.0986)
    return values.astype(jnp.bfloat16)


def draw_cotangent(key, part):
    key = jax.random.fold_in(key, 23)
    values = scaled_normal(key, TOKENS, COLS, 0.0)
    return values.astype(jnp.bfloat16)


def shard_levels(key, dims, pieces, least, largest):
    gain, own = 1.0, jax.random.fold_in(key, 6)
    for dim, parts in pieces:
        heights = jnp.exp(jax.random.uniform(jax.random.fold_in(own, dim), (parts,), jnp.float32, least / len(pieces), largest / len(pieces)))
        gain = gain * jnp.repeat(heights, dims[dim] // parts).reshape([-1 if axis == dim else 1 for axis in range(len(dims))])
    return gain


def bell_draw(rng, shape, deviation, bound, cuts=(), kind=jnp.bfloat16):
    factor_of = shard_levels(rng, shape, cuts, -0.22, 0.18) if cuts else 1.0
    array = jax.random.normal(rng, shape, jnp.float32) * deviation * factor_of
    return jnp.minimum(jnp.maximum(array, -bound), bound).astype(kind)


def setup_inputs(seed: int = 0) -> dict:
    keys = jax.random.split(jax.random.key(seed), 6)
    features = draw_features(jax.random.fold_in(keys[5], 71), 0)
    cotangent = draw_cotangent(jax.random.fold_in(keys[5], 71), 0)
    master = bell_draw(keys[2], (D, COLS), 1.0, 6.0, ((0, 8), (1, 4)), jnp.float32)
    first = bell_draw(keys[3], (D, COLS), 0.5, 3.0, ((0, 8), (1, 4)), jnp.float32)
    second = jnp.clip(jnp.exp(math.log(2.0) - 3.6888794 * jax.random.uniform(keys[4], (D, COLS), jnp.float32) ** shard_levels(keys[4], (D, COLS), ((0, 8), (1, 4)), -0.2, 0.2)), 0.05, 2.0)
    return {"features": features, "cotangent": cotangent, "master": master, "first": first, "second": second}


beta_one = 0.9
beta_two = 0.95
bias_first = 1.0 - 0.9 ** 20
bias_second = 1.0 - 0.95 ** 20
adam_eps = 1e-08
norm_eps = 1e-06
clip_level = 1.0
learn_rate = 0.01
weight_decay = 0.1

def reference(features, cotangent, master, first, second):
    feat_blocks = features.reshape(-1, TOK_DEV, D)
    cot_blocks = cotangent.reshape(-1, TOK_DEV, COLS)

    def accumulate(total, pair):
        left, right = pair
        term = jnp.dot(left.astype(jnp.float32).T, right.astype(jnp.float32), precision=lax.Precision.HIGHEST)
        return (total + term, None)
    grad, _ = lax.scan(accumulate, jnp.zeros((D, COLS), jnp.float32), (feat_blocks, cot_blocks))
    mean_square = jnp.sum(grad * grad) / (D * COLS)
    clip = jnp.minimum(1.0, clip_level / jnp.sqrt(mean_square + norm_eps))
    clipped = clip * grad
    new_first = beta_one * first + (1.0 - beta_one) * clipped
    new_second = beta_two * second + (1.0 - beta_two) * clipped * clipped
    update = new_first / bias_first / (jnp.sqrt(new_second / bias_second) + adam_eps)
    new_master = master - learn_rate * (update + weight_decay * master)
    return (new_master, new_first, new_second)
```

```python
import jax
import jax.numpy as jnp
from jax import lax
from jax.sharding import PartitionSpec as P

D = 8192

beta_one = 0.9
beta_two = 0.95
bias_first = 1.0 - 0.9**20
bias_second = 1.0 - 0.95**20
adam_eps = 1e-08
norm_eps = 1e-06
clip_level = 1.0
learn_rate = 0.01
weight_decay = 0.1

EVERY = ("tensor", "dp", "replica")
LINK = jnp.float16
LINK_TOP = 60000.0


def contract_tokens(left, right):
    return lax.dot_general(
        left, right, (((0,), (0,)), ((), ())), preferred_element_type=jnp.float32
    )


def swap(x, axis):
    return lax.all_to_all(x, axis, split_axis=0, concat_axis=0, tiled=True)


def spread(value, axis):
    count = lax.axis_size(axis)
    return swap(jnp.broadcast_to(value[None], (count, *value.shape)), axis)


def link_scale(features, cotangent, tokens):
    feat_top = jnp.max(jnp.abs(features)).astype(jnp.float32)
    cot_top = jnp.max(jnp.abs(cotangent)).astype(jnp.float32)
    lane = lax.broadcasted_iota(jnp.int32, (1, 128), 1)
    tops = spread(jnp.where(lane == 0, feat_top, cot_top), EVERY)
    tops = jnp.max(tops, axis=(0, 1))
    bound = jnp.maximum(tops[0] * tops[1] * tokens, 1e-30)
    return LINK_TOP / bound, bound / LINK_TOP


def body(features, cotangent, master, first, second):
    tensor, dp, replica = (lax.axis_size(a) for a in EVERY)
    cols = cotangent.shape[1]
    total_cols = cols * tensor
    rows = features.shape[1]
    halves = dp // tensor
    part = rows // halves // replica
    down, up = link_scale(features, cotangent, features.shape[0] * dp * replica)
    all_cols = lax.all_gather(cotangent, "tensor", axis=1, tiled=True)

    partial = contract_tokens(features, all_cols) * down
    partial = partial.astype(LINK).reshape(halves, replica, part, total_cols)
    got = swap(partial.transpose(1, 0, 2, 3), "replica")
    mine = jnp.sum(got.astype(jnp.float32), axis=0)
    mine = mine.astype(LINK).reshape(halves, part, tensor, cols)
    got = swap(mine.transpose(0, 2, 1, 3).reshape(dp, part, cols), "dp")
    fine = jnp.sum(got.astype(jnp.float32), axis=0) * up

    to_owner = [
        (t * dp + h * tensor + c, c * dp + halves * t + h)
        for t in range(tensor)
        for h in range(halves)
        for c in range(tensor)
    ]
    moved = lax.ppermute(fine, ("tensor", "dp"), to_owner)
    squares = spread(jnp.broadcast_to(jnp.sum(fine * fine), (1, 128)), ("tensor", "dp"))
    squares = jnp.broadcast_to(jnp.sum(squares, axis=(0, 1))[:1], (8, cols))
    told = spread(jnp.concatenate([moved, squares], axis=0), "replica")
    grad = told[:, :part].reshape(replica * part, cols)
    square_sum = jnp.sum(told[:, part, 0])

    mean_square = square_sum / (D * total_cols)
    clip = jnp.minimum(1.0, clip_level / jnp.sqrt(mean_square + norm_eps))
    clipped = clip * grad
    new_first = beta_one * first + (1.0 - beta_one) * clipped
    new_second = beta_two * second + (1.0 - beta_two) * clipped * clipped
    update = new_first / bias_first / (jnp.sqrt(new_second / bias_second) + adam_eps)
    new_master = master - learn_rate * (update + weight_decay * master)
    return (new_master, new_first, new_second)


def solution(mesh):
    in_specs = (
        P(("dp", "replica"), "tensor"),
        P(("dp", "replica"), "tensor"),
        P("dp", "tensor"),
        P("dp", "tensor"),
        P("dp", "tensor"),
    )
    out_specs = (P("dp", "tensor"), P("dp", "tensor"), P("dp", "tensor"))
    return jax.shard_map(body, mesh=mesh, in_specs=in_specs, out_specs=out_specs, check_vma=False)
```

```python
import jax
import jax.numpy as jnp
from jax import lax
from jax.sharding import PartitionSpec as P

D = 8192

beta_one = 0.9
beta_two = 0.95
bias_first = 1.0 - 0.9**20
bias_second = 1.0 - 0.95**20
adam_eps = 1e-08
norm_eps = 1e-06
clip_level = 1.0
learn_rate = 0.01
weight_decay = 0.1

EVERY = ("tensor", "dp", "replica")
SUMMED = ("dp", "replica")
LINK = jnp.float16
LINK_TOP = 60000.0
LEAST = 1e-30
LANES = 128
F32 = jnp.float32


def contract_tokens(left, right):
    return lax.dot_general(
        left, right, (((0,), (0,)), ((), ())), preferred_element_type=F32
    )


def swap(x, axis, groups=None):
    return lax.all_to_all(x, axis, split_axis=0, concat_axis=0, axis_index_groups=groups, tiled=True)


def spread(value, axis, count, groups=None):
    return swap(jnp.broadcast_to(value[None], (count, *value.shape)), axis, groups)


def partner(x, bit):
    count = lax.axis_size("tensor")
    return lax.ppermute(x, "tensor", [(i, i ^ bit) for i in range(count)])


def top_of(x):
    return jnp.max(jnp.abs(x)).astype(F32)


def body(features, cotangent, master, first, second):
    tensor, dp, replica = (lax.axis_size(a) for a in EVERY)
    tokens, rows = features.shape
    cols = cotangent.shape[1]
    total_cols = cols * tensor
    halves = dp // tensor
    part = rows // halves // replica
    run = halves * replica
    runs = [list(range(i * run, (i + 1) * run)) for i in range(tensor)]
    blocks_of_runs = [[t * dp * replica + i for t in range(tensor) for i in r] for r in runs]
    apart = [[i * halves + h for i in range(tensor)] for h in range(halves)]

    columns = [cotangent] + [partner(cotangent, j) for j in range(1, tensor)]
    columns = jnp.concatenate(columns, axis=1)

    lane = lax.broadcasted_iota(jnp.int32, (1, LANES), 1)
    tops = jnp.where(lane == 0, top_of(features), top_of(cotangent))
    tops = jnp.max(spread(tops, EVERY, tensor * run, blocks_of_runs), axis=(0, 1))
    bound = jnp.maximum(tops[0] * tops[1] * (tokens * run), LEAST)

    partial = (contract_tokens(features, columns) * (LINK_TOP / bound)).astype(LINK)
    got = swap(partial.reshape(run, part, total_cols), SUMMED, runs)
    mine = jnp.sum(got.astype(F32), axis=0) * bound * (1.0 / LINK_TOP)
    blocks = jnp.stack([mine[:, j * cols : (j + 1) * cols] for j in range(tensor)])
    fine = jnp.sum(swap(blocks, "dp", apart), axis=0)

    to_owner = [
        (t * dp + j * halves + h, (t ^ j) * dp + t * halves + h)
        for t in range(tensor)
        for j in range(tensor)
        for h in range(halves)
    ]
    moved = lax.ppermute(fine, ("tensor", "dp"), to_owner)
    squares = jnp.broadcast_to(jnp.sum(fine * fine), (1, LANES))
    squares = spread(squares, ("tensor", "dp"), tensor * dp)
    squares = jnp.broadcast_to(jnp.sum(squares, axis=(0, 1))[:1], (8, cols))
    told = spread(jnp.concatenate([moved, squares], axis=0), "replica", replica)
    grad = told[:, :part].reshape(replica * part, cols)
    square_sum = jnp.sum(told[:, part, 0])

    mean_square = square_sum / (D * total_cols)
    clip = jnp.minimum(1.0, clip_level / jnp.sqrt(mean_square + norm_eps))
    clipped = clip * grad
    new_first = beta_one * first + (1.0 - beta_one) * clipped
    new_second = beta_two * second + (1.0 - beta_two) * clipped * clipped
    update = new_first / bias_first / (jnp.sqrt(new_second / bias_second) + adam_eps)
    new_master = master - learn_rate * (update + weight_decay * master)
    return (new_master, new_first, new_second)


def solution(mesh):
    in_specs = (
        P(("dp", "replica"), "tensor"),
        P(("dp", "replica"), "tensor"),
        P("dp", "tensor"),
        P("dp", "tensor"),
        P("dp", "tensor"),
    )
    out_specs = (P("dp", "tensor"), P("dp", "tensor"), P("dp", "tensor"))
    return jax.shard_map(body, mesh=mesh, in_specs=in_specs, out_specs=out_specs, check_vma=False)
```

```python
import functools
import math

import jax
import jax.numpy as jnp
from jax import lax
from jax.experimental import pallas as pl
from jax.experimental.pallas import tpu as pltpu
from jax.sharding import PartitionSpec as P

D = 8192

beta_one = 0.9
beta_two = 0.95
bias_first = 1.0 - 0.9**20
bias_second = 1.0 - 0.95**20
adam_eps = 1e-08
norm_eps = 1e-06
clip_level = 1.0
learn_rate = 0.01
weight_decay = 0.1

EVERY = ("tensor", "dp", "replica")
SUMMED = ("dp", "replica")
LINK = jnp.float16
LINK_TOP = 60000.0
LEAST = 1e-30
LANES = 128
TOLD = 8
F32 = jnp.float32
SMALL = pltpu.CompilerParams(vmem_limit_bytes=4 * 2**20)
WHOLE = pl.BlockSpec(memory_space=pltpu.VMEM)


def contract_tokens(left, right):
    return lax.dot_general(
        left, right, (((0,), (0,)), ((), ())), preferred_element_type=F32
    )


def swap(x, axis, groups=None):
    return lax.all_to_all(x, axis, split_axis=0, concat_axis=0, axis_index_groups=groups, tiled=True)


def spread(value, axis, count, groups=None):
    return swap(jnp.broadcast_to(value[None], (count, *value.shape)), axis, groups)


def partner(x, bit):
    count = lax.axis_size("tensor")
    return lax.ppermute(x, "tensor", [(i, i ^ bit) for i in range(count)])


def tops_kernel(features_ref, cotangent_ref, out_ref):
    feat_top = jnp.max(jnp.max(jnp.abs(features_ref[...]).reshape(-1, 16, features_ref.shape[1]), axis=0).astype(F32))
    cot_top = jnp.max(jnp.max(jnp.abs(cotangent_ref[...]).reshape(-1, 16, cotangent_ref.shape[1]), axis=0).astype(F32))
    lane = lax.broadcasted_iota(jnp.int32, out_ref.shape, 2)
    out_ref[...] = jnp.where(lane == 0, feat_top, cot_top)


def tops_of(features, cotangent, count):
    return pl.pallas_call(
        tops_kernel,
        in_specs=[WHOLE] * 2,
        out_specs=WHOLE,
        out_shape=jax.ShapeDtypeStruct((count, 1, LANES), F32),
        compiler_params=pltpu.CompilerParams(vmem_limit_bytes=16 * 2**20),
        cost_estimate=pl.CostEstimate(flops=2 * features.size, bytes_accessed=2 * features.size, transcendentals=0),
        name="tops",
    )(features, cotangent)


def scale_kernel(terms, tops_ref, down_ref, exponent_ref):
    tops = jnp.max(tops_ref[...], axis=0)
    lane = lax.broadcasted_iota(jnp.int32, tops.shape, 1)
    feat_top = jnp.max(jnp.where(lane == 0, tops, 0.0))
    cot_top = jnp.max(jnp.where(lane == 0, 0.0, tops))
    bound = jnp.maximum(jnp.full((8, LANES), feat_top) * cot_top * terms, LEAST)
    exponent = jnp.ceil(jnp.log2(bound * (1.0 / LINK_TOP)))
    down_ref[...] = jnp.exp2(-exponent)[:1, :1]
    exponent_ref[...] = exponent[:1, :1]


def scale_for(tops, terms):
    one = jax.ShapeDtypeStruct((1, 1), F32)
    down, exponent = pl.pallas_call(
        functools.partial(scale_kernel, terms),
        in_specs=[WHOLE],
        out_specs=[WHOLE] * 2,
        out_shape=[one, one],
        compiler_params=SMALL,
        name="scale",
    )(tops)
    return down.reshape(()), exponent.reshape(())


def squares_kernel(fine_ref, out_ref):
    out_ref[...] = jnp.full(out_ref.shape, jnp.sum(fine_ref[...] * fine_ref[...]))


def squares_of(fine, count):
    return pl.pallas_call(
        squares_kernel,
        in_specs=[WHOLE],
        out_specs=WHOLE,
        out_shape=jax.ShapeDtypeStruct((count, 1, LANES), F32),
        compiler_params=SMALL,
        name="squares",
    )(fine)


def pack_kernel(moved_ref, squares_ref, out_ref):
    cols, part = moved_ref.shape
    total = jnp.sum(squares_ref[...], axis=0)
    total = jnp.maximum(jnp.concatenate([total] * (cols // LANES), axis=1), LEAST)
    exponent = jnp.ceil(0.5 * jnp.log2(total) - math.log2(LINK_TOP))
    scale = jnp.exp2(-exponent)
    level = total * scale * scale * LINK_TOP**-2
    high = jnp.floor(level * 2048.0) * (1.0 / 2048.0)
    low = (level - high) * 2048.0
    row = lax.broadcasted_iota(jnp.int32, (TOLD, cols), 0)
    out_ref[:part] = moved_ref[...].T * scale
    out_ref[part:] = jnp.where(row == 0, exponent, jnp.where(row == 1, high, low))


def pack(moved, squares):
    cols, part = moved.shape
    return pl.pallas_call(
        pack_kernel,
        in_specs=[WHOLE] * 2,
        out_specs=WHOLE,
        out_shape=jax.ShapeDtypeStruct((part + TOLD, cols), F32),
        compiler_params=SMALL,
        name="pack",
    )(moved, squares)


def body(features, cotangent, master, first, second):
    tensor, dp, replica = (lax.axis_size(a) for a in EVERY)
    tokens, rows = features.shape
    cols = cotangent.shape[1]
    total_cols = cols * tensor
    halves = dp // tensor
    part = rows // halves // replica
    run = halves * replica
    runs = [list(range(i * run, (i + 1) * run)) for i in range(tensor)]
    blocks_of_runs = [[t * dp * replica + i for t in range(tensor) for i in r] for r in runs]
    apart = [[i * halves + h for i in range(tensor)] for h in range(halves)]

    columns = [cotangent] + [partner(cotangent, j) for j in range(1, tensor)]
    columns = jnp.concatenate(columns, axis=1)

    tops = swap(tops_of(features, cotangent, tensor * run), EVERY, blocks_of_runs)
    down, exponent = scale_for(tops, tokens * run)

    partial = (contract_tokens(columns, features) * down).astype(LINK)
    partial = partial.reshape(total_cols, run, part).transpose(1, 0, 2)
    mine = jnp.sum(swap(partial, SUMMED, runs).astype(F32), axis=0).reshape(tensor, cols, part)
    note = exponent + 0.0 * mine[:, :TOLD]
    message = jnp.concatenate([mine, note], axis=1).astype(LINK)
    got = swap(message, "dp", apart).astype(F32)
    fine = jnp.sum(got[:, :cols] * jnp.exp2(got[:, cols : cols + 1]), axis=0)

    to_owner = [
        (t * dp + j * halves + h, (t ^ j) * dp + t * halves + h)
        for t in range(tensor)
        for j in range(tensor)
        for h in range(halves)
    ]
    moved = lax.ppermute(fine, ("tensor", "dp"), to_owner)
    squares = swap(squares_of(fine, tensor * dp), ("tensor", "dp"))
    told = spread(pack(moved, squares).astype(LINK), "replica", replica).astype(F32)
    factors = jnp.exp2(told[:, part : part + 1])
    halfway = told[:, part + 1 : part + 2] + told[:, part + 2 : part + 3] * (1.0 / 2048.0)
    square_sum = jnp.sum(halfway * factors * factors, axis=0) * LINK_TOP**2
    grad = (told[:, :part] * factors).reshape(replica * part, cols)

    mean_square = square_sum / (D * total_cols)
    clip = jnp.minimum(1.0, clip_level / jnp.sqrt(mean_square + norm_eps))
    clipped = clip * grad
    new_first = beta_one * first + (1.0 - beta_one) * clipped
    new_second = beta_two * second + (1.0 - beta_two) * clipped * clipped
    update = new_first / bias_first / (jnp.sqrt(new_second / bias_second) + adam_eps)
    new_master = master - learn_rate * (update + weight_decay * master)
    return (new_master, new_first, new_second)


def solution(mesh):
    in_specs = (
        P(("dp", "replica"), "tensor"),
        P(("dp", "replica"), "tensor"),
        P("dp", "tensor"),
        P("dp", "tensor"),
        P("dp", "tensor"),
    )
    out_specs = (P("dp", "tensor"), P("dp", "tensor"), P("dp", "tensor"))
    return jax.shard_map(body, mesh=mesh, in_specs=in_specs, out_specs=out_specs, check_vma=False)
```

```python
import functools
import math

import jax
import jax.numpy as jnp
from jax import lax
from jax.experimental import pallas as pl
from jax.experimental.pallas import tpu as pltpu
from jax.sharding import PartitionSpec as P

D = 8192

beta_one = 0.9
beta_two = 0.95
bias_first = 1.0 - 0.9**20
bias_second = 1.0 - 0.95**20
adam_eps = 1e-08
norm_eps = 1e-06
clip_level = 1.0
learn_rate = 0.01
weight_decay = 0.1

EVERY = ("tensor", "dp", "replica")
LINK = jnp.float16
LINK_TOP = 60000.0
LEAST = 1e-30
LANES = 128
TOLD = 8
F32 = jnp.float32
SMALL = pltpu.CompilerParams(vmem_limit_bytes=4 * 2**20)
WHOLE = pl.BlockSpec(memory_space=pltpu.VMEM)


def contract_tokens(left, right):
    return lax.dot_general(
        left, right, (((0,), (0,)), ((), ())), preferred_element_type=F32
    )


def swap(x, axis, groups=None):
    return lax.all_to_all(x, axis, split_axis=0, concat_axis=0, axis_index_groups=groups, tiled=True)


def spread(value, axis, count, groups=None):
    return swap(jnp.broadcast_to(value[None], (count, *value.shape)), axis, groups)


def partner(x, bit):
    count = lax.axis_size("tensor")
    return lax.ppermute(x, "tensor", [(i, i ^ bit) for i in range(count)])


def tops_kernel(features_ref, cotangent_ref, out_ref):
    feat_top = jnp.max(jnp.max(jnp.abs(features_ref[...]).reshape(-1, 16, features_ref.shape[1]), axis=0).astype(F32))
    cot_top = jnp.max(jnp.max(jnp.abs(cotangent_ref[...]).reshape(-1, 16, cotangent_ref.shape[1]), axis=0).astype(F32))
    lane = lax.broadcasted_iota(jnp.int32, out_ref.shape, 2)
    out_ref[...] = jnp.where(lane == 0, feat_top, cot_top)


def tops_of(features, cotangent, count):
    return pl.pallas_call(
        tops_kernel,
        in_specs=[WHOLE] * 2,
        out_specs=WHOLE,
        out_shape=jax.ShapeDtypeStruct((count, 1, LANES), F32),
        compiler_params=pltpu.CompilerParams(vmem_limit_bytes=16 * 2**20),
        cost_estimate=pl.CostEstimate(flops=2 * features.size, bytes_accessed=2 * features.size, transcendentals=0),
        name="tops",
    )(features, cotangent)


def ready_kernel(terms, tops_ref, *refs):
    *blocks, columns_ref, down_ref, exponent_ref = refs
    tops = jnp.max(tops_ref[...], axis=0)
    lane = lax.broadcasted_iota(jnp.int32, tops.shape, 1)
    feat_top = jnp.max(jnp.where(lane == 0, tops, 0.0))
    cot_top = jnp.max(jnp.where(lane == 0, 0.0, tops))
    bound = jnp.maximum(jnp.full((8, LANES), feat_top) * cot_top * terms, LEAST)
    exponent = jnp.ceil(jnp.log2(bound * (1.0 / LINK_TOP)))
    down_ref[...] = jnp.exp2(-exponent)[:1, :1]
    exponent_ref[...] = exponent[:1, :1]
    cols = blocks[0].shape[1]
    me = lax.axis_index("tensor")
    for j, block in enumerate(blocks):
        place = pl.multiple_of((me ^ j) * cols, cols)
        columns_ref[:, pl.ds(place, cols)] = block[...]


def ready(tops, blocks, terms):
    one = jax.ShapeDtypeStruct((1, 1), F32)
    tokens, cols = blocks[0].shape
    columns, down, exponent = pl.pallas_call(
        functools.partial(ready_kernel, terms),
        in_specs=[WHOLE] * (1 + len(blocks)),
        out_specs=[WHOLE] * 3,
        out_shape=[jax.ShapeDtypeStruct((tokens, cols * len(blocks)), blocks[0].dtype), one, one],
        compiler_params=SMALL,
        name="ready",
    )(tops, *blocks)
    return columns, down.reshape(()), exponent.reshape(())


def squares_kernel(fine_ref, out_ref):
    out_ref[...] = jnp.full(out_ref.shape, jnp.sum(fine_ref[...] * fine_ref[...]))


def squares_of(fine, count):
    return pl.pallas_call(
        squares_kernel,
        in_specs=[WHOLE],
        out_specs=WHOLE,
        out_shape=jax.ShapeDtypeStruct((count, 1, LANES), F32),
        compiler_params=SMALL,
        name="squares",
    )(fine)


def pack_kernel(moved_ref, squares_ref, out_ref):
    cols, part = moved_ref.shape
    total = jnp.sum(squares_ref[...], axis=0)
    total = jnp.maximum(jnp.concatenate([total] * (cols // LANES), axis=1), LEAST)
    exponent = jnp.ceil(0.5 * jnp.log2(total) - math.log2(LINK_TOP))
    scale = jnp.exp2(-exponent)
    level = total * scale * scale * LINK_TOP**-2
    high = jnp.floor(level * 2048.0) * (1.0 / 2048.0)
    low = (level - high) * 2048.0
    row = lax.broadcasted_iota(jnp.int32, (TOLD, cols), 0)
    block = moved_ref[...].T * scale
    out_ref[:part] = block * jnp.abs(block) * (1.0 / LINK_TOP)
    out_ref[part:] = jnp.where(row == 0, exponent, jnp.where(row == 1, high, low))


def pack(moved, squares):
    cols, part = moved.shape
    return pl.pallas_call(
        pack_kernel,
        in_specs=[WHOLE] * 2,
        out_specs=WHOLE,
        out_shape=jax.ShapeDtypeStruct((part + TOLD, cols), F32),
        compiler_params=SMALL,
        name="pack",
    )(moved, squares)


def body(features, cotangent, master, first, second):
    tensor, dp, replica = (lax.axis_size(a) for a in EVERY)
    tokens, rows = features.shape
    cols = cotangent.shape[1]
    total_cols = cols * tensor
    halves = dp // tensor
    part = rows // halves // replica
    run = halves * replica
    runs = [[t * dp * replica + i * run + s for s in range(run) for t in range(tensor)] for i in range(tensor)]
    apart = [[i * halves + h for i in range(tensor)] for h in range(halves)]

    blocks = [cotangent] + [partner(cotangent, j) for j in range(1, tensor)]
    tops = swap(tops_of(features, cotangent, tensor * run), EVERY, runs)
    columns, down, exponent = ready(tops, blocks, tokens * run)
    partial = (contract_tokens(columns, features) * down).astype(LINK)
    partial = partial.reshape(total_cols, run, part).transpose(1, 0, 2)
    got = swap(partial.reshape(run * tensor, cols, part), EVERY, runs)
    mine = jnp.sum(got.reshape(run, tensor, cols, part).astype(F32), axis=0)
    note = exponent + 0.0 * mine[:, :TOLD]
    message = jnp.concatenate([mine, note], axis=1).astype(LINK)
    got = swap(message, "dp", apart).astype(F32)
    fine = jnp.sum(got[:, :cols] * jnp.exp2(got[:, cols : cols + 1]), axis=0)

    squares = swap(squares_of(fine, tensor * dp), ("tensor", "dp"))
    told = spread(pack(fine, squares).astype(LINK), "replica", replica).astype(F32)
    factors = jnp.exp2(told[:, part : part + 1])
    halfway = told[:, part + 1 : part + 2] + told[:, part + 2 : part + 3] * (1.0 / 2048.0)
    square_sum = jnp.sum(halfway * factors * factors, axis=0) * LINK_TOP**2
    level = told[:, :part]
    size = jnp.sqrt(jnp.abs(level)) * (factors * LINK_TOP**0.5)
    grad = jnp.where(level < 0.0, -size, size).reshape(replica * part, cols)

    mean_square = square_sum / (D * total_cols)
    clip = jnp.minimum(1.0, clip_level / jnp.sqrt(mean_square + norm_eps))
    clipped = clip * grad
    new_first = beta_one * first + (1.0 - beta_one) * clipped
    new_second = beta_two * second + (1.0 - beta_two) * clipped * clipped
    update = new_first / bias_first / (jnp.sqrt(new_second / bias_second) + adam_eps)
    new_master = master - learn_rate * (update + weight_decay * master)
    return (new_master, new_first, new_second)


def solution(mesh):
    in_specs = (
        P(("dp", "replica"), "tensor"),
        P(("dp", "replica"), "tensor"),
        P("dp", "tensor"),
        P("dp", "tensor"),
        P("dp", "tensor"),
    )
    out_specs = (P("dp", "tensor"), P("dp", "tensor"), P("dp", "tensor"))
    return jax.shard_map(body, mesh=mesh, in_specs=in_specs, out_specs=out_specs, check_vma=False)
```

```python
import functools
import math

import jax
import jax.numpy as jnp
from jax import lax
from jax.experimental import pallas as pl
from jax.experimental.pallas import tpu as pltpu
from jax.sharding import PartitionSpec as P

D = 8192

beta_one = 0.9
beta_two = 0.95
bias_first = 1.0 - 0.9**20
bias_second = 1.0 - 0.95**20
adam_eps = 1e-08
norm_eps = 1e-06
clip_level = 1.0
learn_rate = 0.01
weight_decay = 0.1

EVERY = ("tensor", "dp", "replica")
LINK = jnp.float16
LINK_TOP = 60000.0
LEAST = 1e-30
LANES = 128
TOLD = 8
F32 = jnp.float32
SMALL = pltpu.CompilerParams(vmem_limit_bytes=4 * 2**20)
WHOLE = pl.BlockSpec(memory_space=pltpu.VMEM)


def contract_tokens(left, right):
    return lax.dot_general(
        left, right, (((0,), (0,)), ((), ())), preferred_element_type=F32
    )


def swap(x, axis, groups=None):
    return lax.all_to_all(x, axis, split_axis=0, concat_axis=0, axis_index_groups=groups, tiled=True)


def spread(value, axis, count, groups=None):
    return swap(jnp.broadcast_to(value[None], (count, *value.shape)), axis, groups)


def partner(x, bit):
    count = lax.axis_size("tensor")
    return lax.ppermute(x, "tensor", [(i, i ^ bit) for i in range(count)])


def top_of(ref):
    return jnp.max(jnp.max(jnp.abs(ref[...]).reshape(-1, 16, ref.shape[1]), axis=0).astype(F32))


def own_kernel(features_ref, own_ref, copy_ref, top_ref):
    copy_ref[...] = own_ref[...]
    top_ref[...] = jnp.full(top_ref.shape, top_of(features_ref))


def columns_kernel(top_ref, *refs):
    *blocks, columns_ref, down_ref, exponent_ref = refs
    tokens, cols = blocks[0].shape
    me = lax.axis_index("tensor")
    for j, block in enumerate(blocks):
        place = pl.multiple_of((me ^ j) * cols, cols)
        columns_ref[:, pl.ds(place, cols)] = block[...]
    cot_top = functools.reduce(jnp.maximum, [top_of(block) for block in blocks])
    bound = jnp.maximum(top_ref[...] * cot_top * tokens, LEAST)
    exponent = jnp.ceil(jnp.log2(bound * (1.0 / LINK_TOP)))
    down_ref[...] = jnp.exp2(-exponent)[:1, :1]
    exponent_ref[...] = exponent[:1, :1]


def own_part(features, own):
    return pl.pallas_call(
        own_kernel,
        in_specs=[WHOLE] * 2,
        out_specs=[WHOLE] * 2,
        out_shape=[
            jax.ShapeDtypeStruct(own.shape, own.dtype),
            jax.ShapeDtypeStruct((8, LANES), F32),
        ],
        compiler_params=pltpu.CompilerParams(vmem_limit_bytes=16 * 2**20),
        cost_estimate=pl.CostEstimate(flops=2 * features.size, bytes_accessed=2 * features.size, transcendentals=0),
        name="own",
    )(features, own)


def whole_columns(top, blocks):
    one = jax.ShapeDtypeStruct((1, 1), F32)
    tokens, cols = blocks[0].shape
    columns, down, exponent = pl.pallas_call(
        columns_kernel,
        in_specs=[WHOLE] * (1 + len(blocks)),
        out_specs=[WHOLE] * 3,
        out_shape=[jax.ShapeDtypeStruct((tokens, cols * len(blocks)), blocks[0].dtype), one, one],
        compiler_params=SMALL,
        name="columns",
    )(top, *blocks)
    return columns, down.reshape(()), exponent.reshape(())


def squares_kernel(fine_ref, out_ref):
    out_ref[...] = jnp.full(out_ref.shape, jnp.sum(fine_ref[...] * fine_ref[...]))


def squares_of(fine, count):
    return pl.pallas_call(
        squares_kernel,
        in_specs=[WHOLE],
        out_specs=WHOLE,
        out_shape=jax.ShapeDtypeStruct((count, 1, LANES), F32),
        compiler_params=SMALL,
        name="squares",
    )(fine)


def pack_kernel(moved_ref, squares_ref, out_ref):
    cols, part = moved_ref.shape
    total = jnp.sum(squares_ref[...], axis=0)
    total = jnp.maximum(jnp.concatenate([total] * (cols // LANES), axis=1), LEAST)
    exponent = jnp.ceil(0.5 * jnp.log2(total) - math.log2(LINK_TOP))
    scale = jnp.exp2(-exponent)
    level = total * scale * scale * LINK_TOP**-2
    high = jnp.floor(level * 2048.0) * (1.0 / 2048.0)
    low = (level - high) * 2048.0
    row = lax.broadcasted_iota(jnp.int32, (TOLD, cols), 0)
    block = moved_ref[...].T * scale
    out_ref[:part] = block * jnp.abs(block) * (1.0 / LINK_TOP)
    out_ref[part:] = jnp.where(row == 0, exponent, jnp.where(row == 1, high, low))


def pack(moved, squares):
    cols, part = moved.shape
    return pl.pallas_call(
        pack_kernel,
        in_specs=[WHOLE] * 2,
        out_specs=WHOLE,
        out_shape=jax.ShapeDtypeStruct((part + TOLD, cols), F32),
        compiler_params=SMALL,
        name="pack",
    )(moved, squares)


def body(features, cotangent, master, first, second):
    tensor, dp, replica = (lax.axis_size(a) for a in EVERY)
    tokens, rows = features.shape
    cols = cotangent.shape[1]
    total_cols = cols * tensor
    halves = dp // tensor
    part = rows // halves // replica
    run = halves * replica
    runs = [[t * dp * replica + i * run + s for s in range(run) for t in range(tensor)] for i in range(tensor)]
    apart = [[i * halves + h for i in range(tensor)] for h in range(halves)]

    near, away = partner(cotangent, 1), partner(cotangent, 2)
    own, top = own_part(features, cotangent)
    away, top = lax.optimization_barrier((away, top))
    columns, down, exponent = whole_columns(top, [own, near, away, partner(away, 1)])

    partial = (contract_tokens(columns, features) * down).astype(LINK)
    partial = partial.reshape(total_cols // TOLD, TOLD, run, part).transpose(2, 0, 1, 3)
    partial = partial.reshape(run, tensor, cols // TOLD, TOLD, part)
    note = jnp.broadcast_to(exponent.astype(LINK), (run, tensor, 1, TOLD, part))
    message = jnp.concatenate([partial, note], axis=2)
    got = swap(message.reshape(run * tensor, cols + TOLD, part), EVERY, runs)
    got = got.reshape(run, tensor, cols + TOLD, part)
    factors = jnp.exp2(got[:, :, cols : cols + 1].astype(F32))
    mine = jnp.sum(got[:, :, :cols].astype(F32) * factors, axis=0)
    exponent = jnp.ceil(jnp.log2(jnp.sum(factors, axis=0)))

    note = jnp.broadcast_to(exponent, (tensor, TOLD, part))
    message = jnp.concatenate([mine * jnp.exp2(-exponent), note], axis=1).astype(LINK)
    got = swap(message, "dp", apart).astype(F32)
    fine = jnp.sum(got[:, :cols] * jnp.exp2(got[:, cols : cols + 1]), axis=0)

    squares = swap(squares_of(fine, tensor * dp), ("tensor", "dp"))
    told = spread(pack(fine, squares).astype(LINK), "replica", replica).astype(F32)
    factors = jnp.exp2(told[:, part : part + 1])
    halfway = told[:, part + 1 : part + 2] + told[:, part + 2 : part + 3] * (1.0 / 2048.0)
    square_sum = jnp.sum(halfway * factors * factors, axis=0) * LINK_TOP**2
    level = told[:, :part]
    size = jnp.sqrt(jnp.abs(level)) * (factors * LINK_TOP**0.5)
    grad = jnp.where(level < 0.0, -size, size).reshape(replica * part, cols)

    mean_square = square_sum / (D * total_cols)
    clip = jnp.minimum(1.0, clip_level / jnp.sqrt(mean_square + norm_eps))
    clipped = clip * grad
    new_first = beta_one * first + (1.0 - beta_one) * clipped
    new_second = beta_two * second + (1.0 - beta_two) * clipped * clipped
    update = new_first / bias_first / (jnp.sqrt(new_second / bias_second) + adam_eps)
    new_master = master - learn_rate * (update + weight_decay * master)
    return (new_master, new_first, new_second)


def solution(mesh):
    in_specs = (
        P(("dp", "replica"), "tensor"),
        P(("dp", "replica"), "tensor"),
        P("dp", "tensor"),
        P("dp", "tensor"),
        P("dp", "tensor"),
    )
    out_specs = (P("dp", "tensor"), P("dp", "tensor"), P("dp", "tensor"))
    return jax.shard_map(body, mesh=mesh, in_specs=in_specs, out_specs=out_specs, check_vma=False)
```

```python
import functools
import math

import jax
import jax.numpy as jnp
from jax import lax
from jax.experimental import pallas as pl
from jax.experimental.pallas import tpu as pltpu
from jax.sharding import PartitionSpec as P

D = 8192

beta_one = 0.9
beta_two = 0.95
bias_first = 1.0 - 0.9**20
bias_second = 1.0 - 0.95**20
adam_eps = 1e-08
norm_eps = 1e-06
clip_level = 1.0
learn_rate = 0.01
weight_decay = 0.1

EVERY = ("tensor", "dp", "replica")
LINK = jnp.float16
LINK_TOP = 60000.0
LEAST = 1e-30
LANES = 128
TOLD = 8
F32 = jnp.float32
SMALL = pltpu.CompilerParams(vmem_limit_bytes=4 * 2**20)
WHOLE = pl.BlockSpec(memory_space=pltpu.VMEM)


def contract_tokens(left, right):
    return lax.dot_general(
        left, right, (((0,), (0,)), ((), ())), preferred_element_type=F32
    )


def swap(x, axis, groups=None):
    return lax.all_to_all(x, axis, split_axis=0, concat_axis=0, axis_index_groups=groups, tiled=True)


def spread(value, axis, count, groups=None):
    return swap(jnp.broadcast_to(value[None], (count, *value.shape)), axis, groups)


def partner(x, bit):
    count = lax.axis_size("tensor")
    return lax.ppermute(x, "tensor", [(i, i ^ bit) for i in range(count)])


def top_of(ref):
    return jnp.max(jnp.max(jnp.abs(ref[...]).reshape(-1, 16, ref.shape[1]), axis=0).astype(F32))


def own_kernel(features_ref, own_ref, copy_ref, top_ref):
    copy_ref[...] = own_ref[...]
    top_ref[...] = jnp.full(top_ref.shape, top_of(features_ref))


def columns_kernel(top_ref, *refs):
    *blocks, columns_ref, down_ref, exponent_ref = refs
    tokens, cols = blocks[0].shape
    me = lax.axis_index("tensor")
    for j, block in enumerate(blocks):
        place = pl.multiple_of((me % 2 ^ j) * cols, cols)
        columns_ref[:, pl.ds(place, cols)] = block[...]
    cot_top = functools.reduce(jnp.maximum, [top_of(block) for block in blocks])
    bound = jnp.maximum(top_ref[...] * cot_top * tokens, LEAST)
    exponent = jnp.ceil(jnp.log2(bound * (1.0 / LINK_TOP)))
    down_ref[...] = jnp.exp2(-exponent)[:1, :1]
    exponent_ref[...] = exponent[:1, :1]


def own_part(features, own):
    return pl.pallas_call(
        own_kernel,
        in_specs=[WHOLE] * 2,
        out_specs=[WHOLE] * 2,
        out_shape=[
            jax.ShapeDtypeStruct(own.shape, own.dtype),
            jax.ShapeDtypeStruct((8, LANES), F32),
        ],
        compiler_params=pltpu.CompilerParams(vmem_limit_bytes=16 * 2**20),
        cost_estimate=pl.CostEstimate(flops=2 * features.size, bytes_accessed=2 * features.size, transcendentals=0),
        name="own",
    )(features, own)


def pair_of_columns(top, blocks):
    one = jax.ShapeDtypeStruct((1, 1), F32)
    tokens, cols = blocks[0].shape
    columns, down, exponent = pl.pallas_call(
        columns_kernel,
        in_specs=[WHOLE] * (1 + len(blocks)),
        out_specs=[WHOLE] * 3,
        out_shape=[jax.ShapeDtypeStruct((tokens, cols * len(blocks)), blocks[0].dtype), one, one],
        compiler_params=SMALL,
        name="columns",
    )(top, *blocks)
    return columns, down.reshape(()), exponent.reshape(())


def squares_kernel(fine_ref, out_ref):
    out_ref[...] = jnp.full(out_ref.shape, jnp.sum(fine_ref[...] * fine_ref[...]))


def squares_of(fine, count):
    return pl.pallas_call(
        squares_kernel,
        in_specs=[WHOLE],
        out_specs=WHOLE,
        out_shape=jax.ShapeDtypeStruct((count, 1, LANES), F32),
        compiler_params=SMALL,
        name="squares",
    )(fine)


def pack_kernel(moved_ref, squares_ref, out_ref):
    cols, part = moved_ref.shape
    total = jnp.sum(squares_ref[...], axis=0)
    total = jnp.maximum(jnp.concatenate([total] * (cols // LANES), axis=1), LEAST)
    exponent = jnp.ceil(0.5 * jnp.log2(total) - math.log2(LINK_TOP))
    scale = jnp.exp2(-exponent)
    level = total * scale * scale * LINK_TOP**-2
    high = jnp.floor(level * 2048.0) * (1.0 / 2048.0)
    low = (level - high) * 2048.0
    row = lax.broadcasted_iota(jnp.int32, (TOLD, cols), 0)
    block = moved_ref[...].T * scale
    out_ref[:part] = block * jnp.abs(block) * (1.0 / LINK_TOP)
    out_ref[part:] = jnp.where(row == 0, exponent, jnp.where(row == 1, high, low))


def pack(moved, squares):
    cols, part = moved.shape
    return pl.pallas_call(
        pack_kernel,
        in_specs=[WHOLE] * 2,
        out_specs=WHOLE,
        out_shape=jax.ShapeDtypeStruct((part + TOLD, cols), F32),
        compiler_params=SMALL,
        name="pack",
    )(moved, squares)


def body(features, cotangent, master, first, second):
    tensor, dp, replica = (lax.axis_size(a) for a in EVERY)
    tokens, rows = features.shape
    cols = cotangent.shape[1]
    total_cols = cols * tensor
    halves = dp // tensor
    part = rows // halves // replica
    pair = 2
    run = halves * replica
    runs = [[t * dp * replica + i * run + s for s in range(run) for t in range(tensor)] for i in range(tensor)]
    apart = [[i * halves + h for i in range(tensor)] for h in range(halves)]

    def messages(top, blocks):
        columns, down, exponent = pair_of_columns(top, blocks)
        partial = (contract_tokens(columns, features) * down).astype(LINK)
        partial = partial.reshape(-1, TOLD, run, part).transpose(2, 0, 1, 3)
        partial = partial.reshape(run, len(blocks), cols // TOLD, TOLD, part)
        note = jnp.broadcast_to(exponent.astype(LINK), (run, len(blocks), 1, TOLD, part))
        return jnp.concatenate([partial, note], axis=2)

    near, away = partner(cotangent, 1), partner(cotangent, 2)
    own, top = own_part(features, cotangent)
    chip = lax.axis_index("tensor") // pair
    message = jnp.zeros((run, pair, pair, cols // TOLD + 1, TOLD, part), LINK)
    message = lax.dynamic_update_slice(message, messages(top, [own, near])[:, None], (0, chip, 0, 0, 0, 0))
    away, message = lax.optimization_barrier((away, message))
    far = messages(top, [away, partner(away, 1)])
    message = lax.dynamic_update_slice(message, far[:, None], (0, 1 - chip, 0, 0, 0, 0))
    got = swap(message.reshape(run * tensor, cols + TOLD, part), EVERY, runs)
    got = got.reshape(run, tensor, cols + TOLD, part)
    factors = jnp.exp2(got[:, :, cols : cols + 1].astype(F32))
    mine = jnp.sum(got[:, :, :cols].astype(F32) * factors, axis=0)
    exponent = jnp.ceil(jnp.log2(jnp.sum(factors, axis=0)))

    note = jnp.broadcast_to(exponent, (tensor, TOLD, part))
    message = jnp.concatenate([mine * jnp.exp2(-exponent), note], axis=1).astype(LINK)
    got = swap(message, "dp", apart).astype(F32)
    fine = jnp.sum(got[:, :cols] * jnp.exp2(got[:, cols : cols + 1]), axis=0)

    squares = swap(squares_of(fine, tensor * dp), ("tensor", "dp"))
    told = spread(pack(fine, squares).astype(LINK), "replica", replica).astype(F32)
    factors = jnp.exp2(told[:, part : part + 1])
    halfway = told[:, part + 1 : part + 2] + told[:, part + 2 : part + 3] * (1.0 / 2048.0)
    square_sum = jnp.sum(halfway * factors * factors, axis=0) * LINK_TOP**2
    level = told[:, :part]
    size = jnp.sqrt(jnp.abs(level)) * (factors * LINK_TOP**0.5)
    grad = jnp.where(level < 0.0, -size, size).reshape(replica * part, cols)

    mean_square = square_sum / (D * total_cols)
    clip = jnp.minimum(1.0, clip_level / jnp.sqrt(mean_square + norm_eps))
    clipped = clip * grad
    new_first = beta_one * first + (1.0 - beta_one) * clipped
    new_second = beta_two * second + (1.0 - beta_two) * clipped * clipped
    update = new_first / bias_first / (jnp.sqrt(new_second / bias_second) + adam_eps)
    new_master = master - learn_rate * (update + weight_decay * master)
    return (new_master, new_first, new_second)


def solution(mesh):
    in_specs = (
        P(("dp", "replica"), "tensor"),
        P(("dp", "replica"), "tensor"),
        P("dp", "tensor"),
        P("dp", "tensor"),
        P("dp", "tensor"),
    )
    out_specs = (P("dp", "tensor"), P("dp", "tensor"), P("dp", "tensor"))
    return jax.shard_map(body, mesh=mesh, in_specs=in_specs, out_specs=out_specs, check_vma=False)
```

```python
import functools
import math

import jax
import jax.numpy as jnp
from jax import lax
from jax.experimental import pallas as pl
from jax.experimental.pallas import tpu as pltpu
from jax.sharding import PartitionSpec as P

D = 8192

beta_one = 0.9
beta_two = 0.95
bias_first = 1.0 - 0.9**20
bias_second = 1.0 - 0.95**20
adam_eps = 1e-08
norm_eps = 1e-06
clip_level = 1.0
learn_rate = 0.01
weight_decay = 0.1

EVERY = ("tensor", "dp", "replica")
LINK = jnp.float16
LINK_TOP = 60000.0
LEAST = 1e-30
LANES = 128
TOLD = 8
F32 = jnp.float32
SMALL = pltpu.CompilerParams(vmem_limit_bytes=4 * 2**20)
WHOLE = pl.BlockSpec(memory_space=pltpu.VMEM)


def contract_tokens(left, right):
    return lax.dot_general(
        left, right, (((0,), (0,)), ((), ())), preferred_element_type=F32
    )


def swap(x, axis, groups=None):
    return lax.all_to_all(x, axis, split_axis=0, concat_axis=0, axis_index_groups=groups, tiled=True)


def spread(value, axis, count, groups=None):
    return swap(jnp.broadcast_to(value[None], (count, *value.shape)), axis, groups)


def partner(x, bit):
    count = lax.axis_size("tensor")
    return lax.ppermute(x, "tensor", [(i, i ^ bit) for i in range(count)])


def top_of(ref):
    return jnp.max(jnp.max(jnp.abs(ref[...]).reshape(-1, 16, ref.shape[1]), axis=0).astype(F32))


def own_kernel(features_ref, own_ref, copy_ref, top_ref):
    copy_ref[...] = own_ref[...]
    top_ref[...] = jnp.full(top_ref.shape, top_of(features_ref))


def columns_kernel(top_ref, *refs):
    *blocks, columns_ref, down_ref, exponent_ref = refs
    tokens, cols = blocks[0].shape
    me = lax.axis_index("tensor")
    for j, block in enumerate(blocks):
        place = pl.multiple_of((me % 2 ^ j) * cols, cols)
        columns_ref[:, pl.ds(place, cols)] = block[...]
    cot_top = functools.reduce(jnp.maximum, [top_of(block) for block in blocks])
    bound = jnp.maximum(top_ref[...] * cot_top * tokens, LEAST)
    exponent = jnp.ceil(jnp.log2(bound * (1.0 / LINK_TOP)))
    down_ref[...] = jnp.exp2(-exponent)[:1, :1]
    exponent_ref[...] = exponent[:1, :1]


def own_part(features, own):
    return pl.pallas_call(
        own_kernel,
        in_specs=[WHOLE] * 2,
        out_specs=[WHOLE] * 2,
        out_shape=[
            jax.ShapeDtypeStruct(own.shape, own.dtype),
            jax.ShapeDtypeStruct((8, LANES), F32),
        ],
        compiler_params=pltpu.CompilerParams(vmem_limit_bytes=16 * 2**20),
        cost_estimate=pl.CostEstimate(flops=2 * features.size, bytes_accessed=2 * features.size, transcendentals=0),
        name="own",
    )(features, own)


def pair_of_columns(top, blocks):
    one = jax.ShapeDtypeStruct((1, 1), F32)
    tokens, cols = blocks[0].shape
    columns, down, exponent = pl.pallas_call(
        columns_kernel,
        in_specs=[WHOLE] * (1 + len(blocks)),
        out_specs=[WHOLE] * 3,
        out_shape=[jax.ShapeDtypeStruct((tokens, cols * len(blocks)), blocks[0].dtype), one, one],
        compiler_params=SMALL,
        name="columns",
    )(top, *blocks)
    return columns, down.reshape(()), exponent.reshape(())


def squares_kernel(fine_ref, out_ref):
    out_ref[...] = jnp.full(out_ref.shape, jnp.sum(fine_ref[...] * fine_ref[...]))


def squares_of(fine, count):
    return pl.pallas_call(
        squares_kernel,
        in_specs=[WHOLE],
        out_specs=WHOLE,
        out_shape=jax.ShapeDtypeStruct((count, 1, LANES), F32),
        compiler_params=SMALL,
        name="squares",
    )(fine)


def pack_kernel(moved_ref, squares_ref, out_ref):
    cols, part = moved_ref.shape
    total = jnp.sum(squares_ref[...], axis=0)
    total = jnp.maximum(jnp.concatenate([total] * (cols // LANES), axis=1), LEAST)
    exponent = jnp.ceil(0.5 * jnp.log2(total) - math.log2(LINK_TOP))
    scale = jnp.exp2(-exponent)
    level = total * scale * scale * LINK_TOP**-2
    high = jnp.floor(level * 2048.0) * (1.0 / 2048.0)
    low = (level - high) * 2048.0
    row = lax.broadcasted_iota(jnp.int32, (TOLD, cols), 0)
    block = moved_ref[...].T * scale
    out_ref[:part] = block * jnp.abs(block) * (1.0 / LINK_TOP)
    out_ref[part:] = jnp.where(row == 0, exponent, jnp.where(row == 1, high, low))


def pack(moved, squares):
    cols, part = moved.shape
    return pl.pallas_call(
        pack_kernel,
        in_specs=[WHOLE] * 2,
        out_specs=WHOLE,
        out_shape=jax.ShapeDtypeStruct((part + TOLD, cols), F32),
        compiler_params=SMALL,
        name="pack",
    )(moved, squares)


def body(features, cotangent, master, first, second):
    tensor, dp, replica = (lax.axis_size(a) for a in EVERY)
    tokens, rows = features.shape
    cols = cotangent.shape[1]
    total_cols = cols * tensor
    halves = dp // tensor
    part = rows // halves // replica
    pair = 2
    run = halves * replica
    runs = [[t * dp * replica + i * run + h * replica + r for r in range(replica) for h in range(halves) for t in range(tensor)] for i in range(tensor)]
    apart = [[i * halves + h for i in range(tensor)] for h in range(halves)]

    def messages(top, blocks):
        columns, down, exponent = pair_of_columns(top, blocks)
        partial = (contract_tokens(columns, features) * down).astype(LINK)
        partial = partial.reshape(-1, TOLD, halves, replica, part).transpose(3, 2, 0, 1, 4)
        partial = partial.reshape(run, len(blocks), cols // TOLD, TOLD, part)
        note = jnp.broadcast_to(exponent.astype(LINK), (run, len(blocks), 1, TOLD, part))
        return jnp.concatenate([partial, note], axis=2)

    near, away = partner(cotangent, 1), partner(cotangent, 2)
    own, top = own_part(features, cotangent)
    chip = lax.axis_index("tensor") // pair
    message = jnp.zeros((run, pair, pair, cols // TOLD + 1, TOLD, part), LINK)
    message = lax.dynamic_update_slice(message, messages(top, [own, near])[:, None], (0, chip, 0, 0, 0, 0))
    away, message = lax.optimization_barrier((away, message))
    far = messages(top, [away, partner(away, 1)])
    message = lax.dynamic_update_slice(message, far[:, None], (0, 1 - chip, 0, 0, 0, 0))
    got = swap(message.reshape(run * tensor, cols + TOLD, part), EVERY, runs)
    got = got.reshape(run, tensor, cols + TOLD, part)
    factors = jnp.exp2(got[:, :, cols : cols + 1].astype(F32))
    mine = jnp.sum(got[:, :, :cols].astype(F32) * factors, axis=0)
    exponent = jnp.ceil(jnp.log2(jnp.sum(factors, axis=0)))

    note = jnp.broadcast_to(exponent, (tensor, TOLD, part))
    message = jnp.concatenate([mine * jnp.exp2(-exponent), note], axis=1).astype(LINK)
    got = swap(message, "dp", apart).astype(F32)
    fine = jnp.sum(got[:, :cols] * jnp.exp2(got[:, cols : cols + 1]), axis=0)

    squares = swap(squares_of(fine, tensor * dp), ("tensor", "dp"))
    told = spread(pack(fine, squares).astype(LINK), "replica", replica).astype(F32)
    factors = jnp.exp2(told[:, part : part + 1])
    halfway = told[:, part + 1 : part + 2] + told[:, part + 2 : part + 3] * (1.0 / 2048.0)
    square_sum = jnp.sum(halfway * factors * factors, axis=0) * LINK_TOP**2
    level = told[:, :part]
    size = jnp.sqrt(jnp.abs(level)) * (factors * LINK_TOP**0.5)
    grad = jnp.where(level < 0.0, -size, size).reshape(replica * part, cols)

    mean_square = square_sum / (D * total_cols)
    clip = jnp.minimum(1.0, clip_level / jnp.sqrt(mean_square + norm_eps))
    clipped = clip * grad
    new_first = beta_one * first + (1.0 - beta_one) * clipped
    new_second = beta_two * second + (1.0 - beta_two) * clipped * clipped
    update = new_first / bias_first / (jnp.sqrt(new_second / bias_second) + adam_eps)
    new_master = master - learn_rate * (update + weight_decay * master)
    return (new_master, new_first, new_second)


def solution(mesh):
    in_specs = (
        P(("dp", "replica"), "tensor"),
        P(("dp", "replica"), "tensor"),
        P("dp", "tensor"),
        P("dp", "tensor"),
        P("dp", "tensor"),
    )
    out_specs = (P("dp", "tensor"), P("dp", "tensor"), P("dp", "tensor"))
    return jax.shard_map(body, mesh=mesh, in_specs=in_specs, out_specs=out_specs, check_vma=False)
```
